128 devices in a mesh: dp: 16 (over y, x), tensor: 8 (over z, core).
Axes of the slice: x: 4, y: 4, z: 4, core: 2. Of those that a mesh axis runs over, the one named last changes fastest.
Arguments:
- normed_hidden_rows: bfloat16 [8192, 8192], P('dp', 'tensor'), may hold values from -6 to 6
- frozen_query_base: bfloat16 [8192, 8192], P('dp', 'tensor'), may hold values from -150 to 150
- completion_key_value: bfloat16 [8192, 2, 8, 128], P('dp', None, 'tensor'), may hold values from -7 to 7
- prompt_key_value: bfloat16 [4096, 2, 8, 128], P('dp', None, 'tensor'), may hold values from -6 to 6
- adapter_down_weight: bfloat16 [128, 8192], P(None, 'tensor'), may hold values from -0.0625 to 0.0625
- adapter_up_weight: bfloat16 [128, 8192], P(None, 'tensor'), may hold values from -0.5 to 0.5
- output_gradient: bfloat16 [8192, 8192], P('dp', 'tensor'), may hold values from -6 to 6
- prompt_per_slot: int32 [16], replicated, may hold values from 0 to 3, as said below
- prompt_token_count: int32 [4], replicated, may hold values from 1 to 1024, as said below
- completion_length: int32 [64], P('dp'), may hold values from 1 to 128, as said below
- block_storage_slot: int32 [32], replicated, may hold values from 0 to 31, as said below
Outputs:
- attn_out: bfloat16 [8192, 8192], P('dp', 'tensor')
- grad_down: float32 [128, 8192], P('dp', 'tensor')
- up_weight_gradient: float32 [128, 8192], P('dp', 'tensor')
- d_prompt_kv: float32 [4096, 2, 8, 128], P('dp', None, 'tensor')
- own_key_value_gradient: float32 [8192, 2, 8, 128], P('dp', None, 'tensor')
The draws below stay inside these ranges and needn't reach their ends.
Inputs may be any that keep to these rules, and one draw needn't show every extreme that they name: `prompt_per_slot`: each of the 4 prompts is named by exactly 4 entries. `prompt_token_count`: some prompt has 1024 tokens. `completion_length`: some completion has 128 tokens. `block_storage_slot`: A permutation of the 32 storage slots; the 2 slots d * 2 to d * 2 + 1 hold blocks of distinct prompts.
All inputs are finite; a program needn't handle non-finite values.
Results may differ from the reference program's by a relative error of at most 0.0096.
Values may be sent and summed in bfloat16 or wider, within the bound.
No kernel may reach another device: no remote copies, remote signals or barrier semaphores. Data moves between devices by JAX's collectives and lax.ppermute only.
A program may use at most 128 MiB of HBM per device.

```python
import math
import jax
import jax.numpy as jnp
from jax import lax

MODEL_WIDTH = 8192
QUERY_HEADS = 64
KEY_VALUE_HEADS = 8
HEAD_SIZE = 128
ADAPTER_RANK = 128
C_DEV = 4
BLK_DEV = 2
COMPLETION_SLOTS = 128
LP = 1024
QUERY_PER_KEY = 8
NBP = 8
BLOCK_TOKENS = 128
TOTAL_COMPLETION = 64
TOKEN_SLOTS = 8192
PROMPTS = 4
TOTAL_BLOCKS = 32
N_DP = 16


def shared_keys(key):
    random_base_keys = jnp.clip(jax.random.normal(jax.random.fold_in(key, 101), (TOTAL_COMPLETION, COMPLETION_SLOTS, 2, KEY_VALUE_HEADS, HEAD_SIZE), jnp.float32), -6.0, 6.0)
    return random_base_keys


def draw_completion_key_value(key, part):
    random_base_keys = shared_keys(key)
    tilted_rows = random_base_keys
    return tilted_rows.reshape(TOKEN_SLOTS, 2, KEY_VALUE_HEADS, HEAD_SIZE).astype(jnp.bfloat16)


def draw_frozen_query_base(key, part):
    key = jax.random.fold_in(key, 6)
    drawn_arrays = jnp.clip(jax.random.normal(key, (TOTAL_COMPLETION, COMPLETION_SLOTS, KEY_VALUE_HEADS, QUERY_PER_KEY, HEAD_SIZE), jnp.float32), -6.0, 6.0)
    return drawn_arrays.reshape(TOKEN_SLOTS, QUERY_HEADS * HEAD_SIZE).astype(jnp.bfloat16)


def draw_prompt_per_slot(key, part):
    key = jax.random.fold_in(key, 1)
    shuffled = jax.random.permutation(key, N_DP)
    return (shuffled % PROMPTS).astype(jnp.int32)


def draw_prompt_token_count(key, part):
    key = jax.random.fold_in(key, 2)
    key_lengths, key_longest = jax.random.split(key)
    lengths = jax.random.randint(key_lengths, (PROMPTS,), 1, LP + 1)
    longest = jax.random.randint(key_longest, (), 0, PROMPTS)
    return lengths.at[longest].set(LP).astype(jnp.int32)


def draw_completion_length(key, part):
    key = jax.random.fold_in(key, 3)
    key_lengths, key_longest = jax.random.split(key)
    lengths = jax.random.randint(key_lengths, (TOTAL_COMPLETION,), 1, COMPLETION_SLOTS + 1)
    longest = jax.random.randint(key_longest, (), 0, TOTAL_COMPLETION)
    return lengths.at[longest].set(COMPLETION_SLOTS).astype(jnp.int32)


def draw_block_storage_slot(key, part):
    key = jax.random.fold_in(key, 4)
    key_devices, key_prompts, key_blocks = jax.random.split(key, 3)
    device_order = jax.random.permutation(key_devices, N_DP).astype(jnp.int32)
    prompt_order = jax.random.permutation(key_prompts, PROMPTS).astype(jnp.int32)
    device_ids = jnp.arange(N_DP * BLK_DEV, dtype=jnp.int32) // BLK_DEV
    slot_ids = jnp.arange(N_DP * BLK_DEV, dtype=jnp.int32) % BLK_DEV
    storage = device_order[device_ids] * BLK_DEV + slot_ids
    labels = prompt_order[(device_ids + slot_ids) % PROMPTS]
    tiebreak = jax.random.permutation(key_blocks, TOTAL_BLOCKS).astype(jnp.int32)
    ordering = jnp.argsort(labels * TOTAL_BLOCKS + tiebreak)
    return storage[ordering].astype(jnp.int32)


def steps_of(stream_key, extent, shards, smallest, top_value):
    def one(axis_at, shards_of):
        heights = jax.random.uniform(jax.random.fold_in(jax.random.fold_in(stream_key, 6), axis_at), (shards_of,), jnp.float32, smallest / len(shards), top_value / len(shards))
        return jnp.repeat(jnp.exp(heights), extent[axis_at] // shards_of).reshape((-1,) + (1,) * (len(extent) - axis_at - 1))

    gain = one(*shards[0])
    for cut in shards[1:]:
        gain = gain * one(*cut)
    return gain


def noise(rng, dims, scale, bound, pieces=(), kind=jnp.bfloat16):
    gain = steps_of(rng, dims, pieces, -0.22, 0.18) if pieces else 1.0
    values = jax.random.normal(rng, dims, jnp.float32) * scale * gain
    return jnp.minimum(jnp.maximum(values, -bound), bound).astype(kind)


def setup_inputs(seed: int = 0) -> dict:
    arg_keys = jax.random.split(jax.random.key(seed), 12)
    return {
        "normed_hidden_rows": noise(arg_keys[0], (TOKEN_SLOTS, MODEL_WIDTH), 1.0, 6.0, ((0, 16), (1, 8))),
        "frozen_query_base": draw_frozen_query_base(jax.random.fold_in(arg_keys[11], 71), 0),
        "completion_key_value": draw_completion_key_value(jax.random.fold_in(arg_keys[11], 71), 0),
        "prompt_key_value": noise(arg_keys[3], (TOTAL_BLOCKS * BLOCK_TOKENS, 2, KEY_VALUE_HEADS, HEAD_SIZE), 1.0, 6.0, ((0, 16), (2, 8))),
        "adapter_down_weight": noise(arg_keys[4], (ADAPTER_RANK, MODEL_WIDTH), MODEL_WIDTH ** -0.5, 0.0625, ((1, 8),)),
        "adapter_up_weight": noise(arg_keys[5], (ADAPTER_RANK, QUERY_HEADS * HEAD_SIZE), ADAPTER_RANK ** -0.5, 0.5, ((1, 8),)),
        "output_gradient": noise(arg_keys[6], (TOKEN_SLOTS, QUERY_HEADS * HEAD_SIZE), 1.0, 6.0, ((0, 16), (1, 8))),
        "prompt_per_slot": draw_prompt_per_slot(jax.random.fold_in(arg_keys[11], 71), 0),
        "prompt_token_count": draw_prompt_token_count(jax.random.fold_in(arg_keys[11], 71), 0),
        "completion_length": draw_completion_length(jax.random.fold_in(arg_keys[11], 71), 0),
        "block_storage_slot": draw_block_storage_slot(jax.random.fold_in(arg_keys[11], 71), 0),
    }


rope_base = 1000000.0
adapter_scale = 1.0

def apply_rotary(values, token_positions, turning):
    half_dim = values.shape[-1] // 2
    frequency = rope_base ** (-jnp.arange(half_dim).astype(jnp.float32) * 2.0 / values.shape[-1])
    angles = token_positions.astype(jnp.float32)[:, None] * frequency[None, :]
    cosine = jnp.cos(angles)[:, None, :]
    sine_part = turning * jnp.sin(angles)[:, None, :]
    lower_half = values[..., :half_dim]
    upper_half = values[..., half_dim:]
    return jnp.concatenate([lower_half * cosine - upper_half * sine_part, upper_half * cosine + lower_half * sine_part], axis=-1)

def attend(query_rows, key_rows, value_rows, grad_rows, prompt_length, comp_length):
    n_own = query_rows.shape[0]
    n_keys = key_rows.shape[0]
    n_prompt = n_keys - n_own
    row_ids = jnp.arange(n_own).astype(jnp.int32)[:, None]
    key_ids = jnp.arange(n_keys).astype(jnp.int32)[None, :]
    allowed = jnp.where(key_ids < n_prompt, key_ids < prompt_length, key_ids - n_prompt <= row_ids)
    inv_scale = 1.0 / math.sqrt(query_rows.shape[-1])
    q32 = query_rows.astype(jnp.float32)
    k32 = key_rows.astype(jnp.float32)
    v32 = value_rows.astype(jnp.float32)
    scores = jnp.einsum('tgmd,sgd->gtms', q32, k32) * inv_scale
    scores = jnp.where(allowed[None, :, None, :], scores, -1e+30)
    row_max = lax.optimization_barrier(jnp.max(scores, axis=-1, keepdims=True))
    weights = jnp.exp(scores - row_max)
    probabilities = weights / lax.optimization_barrier(jnp.sum(weights, axis=-1, keepdims=True))
    probs_low = probabilities.astype(jnp.bfloat16)
    p32 = probs_low.astype(jnp.float32)
    live_rows = (jnp.arange(n_own).astype(jnp.int32) < comp_length)[:, None, None, None]
    result = jnp.where(live_rows, jnp.einsum('gtms,sgd->tgmd', p32, v32), 0.0)
    grad_live = jnp.where(live_rows, grad_rows, jnp.zeros_like(grad_rows)).astype(jnp.float32)
    d_probs = jnp.einsum('tgmd,sgd->gtms', grad_live, v32)
    row_dot = lax.optimization_barrier(jnp.sum(probabilities * d_probs, axis=-1, keepdims=True))
    d_scores = (probabilities * (d_probs - row_dot) * inv_scale).astype(jnp.bfloat16).astype(jnp.float32)
    d_query = jnp.einsum('gtms,sgd->tgmd', d_scores, k32)
    d_keys = jnp.einsum('gtms,tgmd->sgd', d_scores, q32)
    d_values = jnp.einsum('gtms,tgmd->sgd', p32, grad_live)
    return (result, d_query, d_keys, d_values)

def reference(normed_hidden_rows, frozen_query_base, completion_key_value, prompt_key_value, adapter_down_weight, adapter_up_weight, output_gradient, prompt_per_slot, prompt_token_count, completion_length, block_storage_slot):
    adapter_middle = jnp.dot(normed_hidden_rows, adapter_down_weight.T, preferred_element_type=jnp.float32).astype(jnp.bfloat16)
    adapter_delta = jnp.dot(adapter_middle, adapter_up_weight, preferred_element_type=jnp.float32)
    comp_prompt = prompt_per_slot[jnp.arange(TOTAL_COMPLETION).astype(jnp.int32) // C_DEV].astype(jnp.int32)
    token_positions = (prompt_token_count[comp_prompt][:, None] + jnp.arange(COMPLETION_SLOTS).astype(jnp.int32)[None, :]).reshape(-1).astype(jnp.int32)
    rotary_applied = apply_rotary(adapter_delta.reshape(TOKEN_SLOTS, QUERY_HEADS, HEAD_SIZE), token_positions, 1.0).reshape(TOKEN_SLOTS, QUERY_HEADS * HEAD_SIZE)
    query_rows = (frozen_query_base.astype(jnp.float32) + adapter_scale * rotary_applied).astype(jnp.bfloat16)
    query_parts = query_rows.reshape(TOTAL_COMPLETION, COMPLETION_SLOTS, KEY_VALUE_HEADS, QUERY_PER_KEY, HEAD_SIZE)
    completion_split = completion_key_value.reshape(TOTAL_COMPLETION, COMPLETION_SLOTS, 2, KEY_VALUE_HEADS, HEAD_SIZE)
    gradient_split = output_gradient.reshape(TOTAL_COMPLETION, COMPLETION_SLOTS, KEY_VALUE_HEADS, QUERY_PER_KEY, HEAD_SIZE)
    token_ids = jnp.arange(LP).astype(jnp.int32)

    def per_completion(d_prompt_acc, member):
        query_one, own_one, grad_one, prompt_one, length_one = member
        token_rows = (block_storage_slot[prompt_one * NBP + token_ids // BLOCK_TOKENS] * BLOCK_TOKENS + token_ids % BLOCK_TOKENS).astype(jnp.int32)
        prompt_rows = jnp.take(prompt_key_value, token_rows, axis=0)
        key_rows = jnp.concatenate([prompt_rows[:, 0], own_one[:, 0]], axis=0)
        value_rows = jnp.concatenate([prompt_rows[:, 1], own_one[:, 1]], axis=0)
        result, d_query, d_keys, d_values = attend(query_one, key_rows, value_rows, grad_one, prompt_token_count[prompt_one], length_one)
        d_kv = jnp.stack([d_keys, d_values], axis=1)
        d_prompt_acc = d_prompt_acc.at[token_rows].add(d_kv[:LP])
        return (d_prompt_acc, (result, d_query, d_kv[LP:]))
    starting_accumulator = jnp.zeros((TOTAL_BLOCKS * BLOCK_TOKENS, 2, KEY_VALUE_HEADS, HEAD_SIZE), jnp.float32)
    d_prompt_kv, (results, d_queries, own_gradient) = lax.scan(per_completion, starting_accumulator, (query_parts, completion_split, gradient_split, comp_prompt, completion_length))
    attn_out = results.reshape(TOKEN_SLOTS, QUERY_HEADS * HEAD_SIZE).astype(jnp.bfloat16)
    query_gradient_total = d_queries.reshape(TOKEN_SLOTS, QUERY_HEADS, HEAD_SIZE)
    delta_gradient = (adapter_scale * apply_rotary(query_gradient_total, token_positions, -1.0)).reshape(TOKEN_SLOTS, QUERY_HEADS * HEAD_SIZE).astype(jnp.bfloat16)
    up_weight_gradient = jnp.dot(adapter_middle.T, delta_gradient, preferred_element_type=jnp.float32)
    middle_gradient = jnp.dot(delta_gradient, adapter_up_weight.T, preferred_element_type=jnp.float32).astype(jnp.bfloat16)
    grad_down = jnp.dot(middle_gradient.T, normed_hidden_rows, preferred_element_type=jnp.float32)
    own_key_value_gradient = own_gradient.reshape(TOKEN_SLOTS, 2, KEY_VALUE_HEADS, HEAD_SIZE)
    return (attn_out, grad_down, up_weight_gradient, d_prompt_kv, own_key_value_gradient)
```

```python
import math

import jax
import jax.numpy as jnp
from jax import lax
from jax.experimental import pallas as pl
from jax.experimental.pallas import tpu as pltpu
from jax.sharding import PartitionSpec as P

ROPE_BASE = 1000000.0
BF = jnp.bfloat16
F32 = jnp.float32
HEAD = 128
SUB = 32
CHUNK = 128
PAIR = 2
SPAN = 256
MIB = 1024 * 1024
VM = pl.BlockSpec(memory_space=pltpu.VMEM)
SM = pl.BlockSpec(memory_space=pltpu.SMEM)
HBM = pl.BlockSpec(memory_space=pltpu.HBM)


def shape(dims, dtype):
    return jax.ShapeDtypeStruct(dims, dtype)


def dot(a, b):
    return jnp.dot(a, b, preferred_element_type=F32)


def dot_nt(a, b):
    return lax.dot_general(a, b, (((1,), (1,)), ((), ())), preferred_element_type=F32)


def call(body, out, in_specs, out_specs, mib, scratch=()):
    return pl.pallas_call(
        body,
        out_shape=out,
        in_specs=in_specs,
        out_specs=out_specs,
        scratch_shapes=list(scratch),
        compiler_params=pltpu.CompilerParams(vmem_limit_bytes=mib * MIB),
    )


def stored_prompts(slots, me, per_prompt):
    first = jnp.int32(0)
    second = jnp.int32(0)
    for j in range(slots.shape[0]):
        slot = slots[j]
        first = jnp.where(slot == 2 * me, j // per_prompt, first)
        second = jnp.where(slot == 2 * me + 1, j // per_prompt, second)
    return first, second


def split_halves(value, send_ref, keep_ref):
    core = lax.rem(lax.axis_index("tensor"), 2)
    half = keep_ref.shape[0]
    send_ref[...] = jnp.where(core == 0, value[half:], value[:half])
    keep_ref[...] = jnp.where(core == 0, value[:half], value[half:])


def join_halves(kept, other, ref):
    core = lax.rem(lax.axis_index("tensor"), 2)
    half = kept.shape[0]
    ref[pl.ds(pl.multiple_of(core * half, half), half), :] = kept[...]
    ref[pl.ds(pl.multiple_of((1 - core) * half, half), half), :] = other[...]


def pack_rows(value, part, ref, first):
    for e in range(ref.shape[0]):
        rows = value[e * part : (e + 1) * part]
        for k in range(value.shape[1] // HEAD // 2):
            left = rows[:, 2 * k * HEAD : (2 * k + 1) * HEAD]
            right = rows[:, (2 * k + 1) * HEAD : (2 * k + 2) * HEAD]
            pair = jnp.concatenate([left, right], axis=0).astype(BF)
            ref[e, first + 2 * k * part : first + 2 * (k + 1) * part] = pair


def unpack_sum(got, part, first, out_ref):
    for k in range(out_ref.shape[1] // HEAD // 2):
        span = slice(first + 2 * k * part, first + 2 * (k + 1) * part)
        pair = got[0, span].astype(F32)
        for e in range(1, got.shape[0]):
            pair += got[e, span].astype(F32)
        out_ref[:, 2 * k * HEAD : (2 * k + 1) * HEAD] = pair[:part]
        out_ref[:, (2 * k + 1) * HEAD : (2 * k + 2) * HEAD] = pair[part:]


def prepare(prompts, counts, slots, hidden, down, stored, mid_send, mid_keep, send_ref, cosine, sine, wide):
    split_halves(dot_nt(hidden[...], down[...]), mid_send, mid_keep)
    n_dp = send_ref.shape[0]
    rows = send_ref.shape[2]
    wide[...] = stored[...].astype(F32)
    per_prompt = slots.shape[0] * 4 // prompts.shape[0]
    _, second = stored_prompts(slots, lax.axis_index("dp"), per_prompt)
    keys = wide[pl.ds(0, 2 * rows, 2), :].astype(BF)
    values = wide[pl.ds(1, 2 * rows, 2), :].astype(BF)
    for e in range(n_dp):
        take = prompts[e] == second
        send_ref[e, 0] = jnp.where(take, keys[rows:], keys[:rows])
        send_ref[e, 1] = jnp.where(take, values[rows:], values[:rows])
    lane = lax.broadcasted_iota(jnp.int32, cosine.shape, 1)
    token = lax.broadcasted_iota(jnp.int32, cosine.shape, 0)
    pair = lax.rem(lane, HEAD // 2).astype(F32)
    frequency = jnp.exp2(pair * (-2.0 / HEAD * math.log2(ROPE_BASE)))
    position = counts[prompts[lax.axis_index("dp")]] + token
    angles = position.astype(F32) * frequency
    cosine[...] = jnp.cos(angles)
    sin = jnp.sin(angles)
    sine[...] = jnp.where(lane < HEAD // 2, -sin, sin)


def prepare_own(lengths, grad, own, g_rows, own_keys, own_values, own_keys_t, own_values_t, wide):
    n_comp, tokens, _ = own_keys.shape
    n_sub = tokens // SUB
    wide[...] = own[...].astype(F32)
    token_ids = lax.broadcasted_iota(jnp.int32, (tokens, HEAD), 0)
    for c in range(n_comp):
        k = wide[pl.ds(2 * c * tokens, tokens, 2), :].astype(BF)
        v = wide[pl.ds(2 * c * tokens + 1, tokens, 2), :].astype(BF)
        own_keys[c] = k
        own_values[c] = v
        own_keys_t[c] = k.T
        own_values_t[c] = v.T
        live = token_ids < lengths[c]
        for h in range(grad.shape[1] // HEAD):
            g = grad[c * tokens : (c + 1) * tokens, h * HEAD : (h + 1) * HEAD].astype(F32)
            g = jnp.where(live, g, 0.0).astype(BF)
            for s in range(n_sub):
                g_rows[c * n_sub + s, h * SUB : (h + 1) * SUB] = g[s * SUB : (s + 1) * SUB]


def attention(
    prompts,
    counts,
    lengths,
    slots,
    mid_kept,
    mid_other,
    base,
    up,
    gathered,
    g_rows,
    own_keys,
    own_values,
    own_keys_t,
    own_values_t,
    cosine,
    sine,
    out_hbm,
    dmid_send,
    dmid_keep,
    dprompt_hbm,
    down_hbm,
    units,
    mid,
    keys,
    values,
    keys_t,
    values_t,
    q_rows,
    scores,
    dprobs,
    probs_low,
    dscores,
    dkeys,
    dvalues,
    own_dkeys,
    own_dvalues,
    ddelta,
    out_ref,
    dprompt_ref,
    down_ref,
    sems,
):
    n_comp = lengths.shape[0]
    tokens = base.shape[0] // n_comp
    heads = base.shape[1] // HEAD
    n_sub = tokens // SUB
    rows = heads * SUB
    n_prompt = keys.shape[0]
    n_keys = n_prompt + tokens
    n_blocks = n_prompt // tokens
    prompt = prompts[lax.axis_index("dp")]
    count = counts[prompt]
    join_halves(mid_kept, mid_other, mid)
    inv_scale = 1.0 / math.sqrt(HEAD)
    exp2_scale = inv_scale * math.log2(math.e)

    dkeys[...] = jnp.zeros_like(dkeys)
    dvalues[...] = jnp.zeros_like(dvalues)
    own_dkeys[...] = jnp.zeros_like(own_dkeys)
    own_dvalues[...] = jnp.zeros_like(own_dvalues)
    out_ref[...] = jnp.zeros_like(out_ref)
    ddelta[...] = jnp.zeros_like(ddelta)
    for j in range(n_blocks):
        source = slots[prompt * n_blocks + j] // 2
        span = slice(j * tokens, (j + 1) * tokens)
        k = gathered[source, 0]
        v = gathered[source, 1]
        keys[span] = k
        values[span] = v
        keys_t[:, span] = k.T
        values_t[:, span] = v.T
    cos = cosine[...]
    sin = sine[...]

    n_live = jnp.int32(0)
    for c in range(n_comp):
        n_live += (lengths[c] + SUB - 1) // SUB
    at_live = jnp.int32(0)
    at_dead = n_live
    for c in range(n_comp):
        for s in range(n_sub):
            live = s * SUB < lengths[c]
            place = jnp.where(live, at_live, at_dead)
            units[place] = c * n_sub + s
            at_live += jnp.where(live, 1, 0)
            at_dead += jnp.where(live, 0, 1)

    for c in range(n_comp):
        span = slice(c * tokens, (c + 1) * tokens)
        delta = dot(mid[span], up[...])
        for h in range(heads):
            cols = slice(h * HEAD, (h + 1) * HEAD)
            d = delta[:, cols]
            turned = d * cos + pltpu.roll(d, HEAD // 2, 1) * sin
            q = (base[span, cols].astype(F32) + turned).astype(BF)
            for s in range(n_sub):
                q_rows[c * n_sub + s, h * SUB : (h + 1) * SUB] = q[s * SUB : (s + 1) * SUB]

    class Unit:
        def __init__(self, n, u, used):
            self.u = u
            self.used = used
            unit = units[n]
            self.c = unit // n_sub
            self.first = (unit % n_sub) * SUB
            self.q = q_rows[unit]
            self.g = g_rows[unit]
            self.q_t = self.q.T
            self.g_t = self.g.T
            self.top = None
            self.total = jnp.zeros((8, rows), F32)
            self.mean = jnp.zeros((8, rows), F32)

        def score(self, at):
            span = slice(at, at + CHUNK)
            key_token = lax.broadcasted_iota(jnp.int32, (CHUNK, rows), 0)
            if at < self.used:
                x = dot(keys[span], self.q_t)
                allowed = key_token < count - at if at >= self.used - SPAN else None
            else:
                x = dot(own_keys[self.c, at - n_prompt : at - n_prompt + CHUNK], self.q_t)
                col_token = self.first + lax.broadcasted_iota(jnp.int32, (CHUNK, rows), 1) % SUB
                allowed = key_token + (at - n_prompt) <= col_token
            if allowed is not None:
                x = jnp.where(allowed, x, -1e30)
            scores[self.u, span] = x
            t = jnp.max(x.reshape(CHUNK // 8, 8, rows), axis=0)
            self.top = t if self.top is None else jnp.maximum(self.top, t)

        def scored(self):
            self.top = jnp.max(self.top, axis=0, keepdims=True)

        def weigh(self, at):
            span = slice(at, at + CHUNK)
            if at < n_prompt:
                dp = dot(values[span], self.g_t)
            else:
                dp = dot(own_values[self.c, at - n_prompt : at - n_prompt + CHUNK], self.g_t)
            w = jnp.exp2((scores[self.u, span] - self.top) * exp2_scale)
            scores[self.u, span] = w
            dprobs[self.u, span] = dp
            self.total += jnp.sum(w.reshape(CHUNK // 8, 8, rows), axis=0)
            self.mean += jnp.sum((w * dp).reshape(CHUNK // 8, 8, rows), axis=0)

        def weighed(self):
            self.inv = 1.0 / jnp.sum(self.total, axis=0, keepdims=True)
            self.mean = jnp.sum(self.mean, axis=0, keepdims=True) * self.inv

        def differ(self, at):
            span = slice(at, at + CHUNK)
            p = scores[self.u, span] * self.inv
            probs_low[self.u, span] = p.astype(BF)
            dscores[self.u, span] = (p * (dprobs[self.u, span] - self.mean)).astype(BF)

        def finish(self):
            u, c = self.u, self.c
            used = self.used
            low = probs_low[u, :used]
            ds = dscores[u, :used]
            own_low = probs_low[u, n_prompt:]
            own_ds = dscores[u, n_prompt:]
            out = (dot(values_t[:, :used], low) + dot(own_values_t[c], own_low)).T
            dq = ((dot(keys_t[:, :used], ds) + dot(own_keys_t[c], own_ds)) * inv_scale).T
            dvalues[:used] += dot(low, self.g)
            dkeys[:used] += dot(ds, self.q)
            own_dvalues[c] += dot(own_low, self.g)
            own_dkeys[c] += dot(own_ds, self.q)
            first = self.first
            at = pl.multiple_of(c * tokens + first, SUB)
            row_live = lax.broadcasted_iota(jnp.int32, (SUB, HEAD), 0) + first < lengths[c]
            c_part = cosine[pl.ds(first, SUB), :]
            s_part = sine[pl.ds(first, SUB), :]
            for h in range(heads):
                cols = slice(h * HEAD, (h + 1) * HEAD)
                o = out[h * SUB : (h + 1) * SUB]
                out_ref[pl.ds(at, SUB), cols] = jnp.where(row_live, o, 0.0).astype(BF)
                d = dq[h * SUB : (h + 1) * SUB]
                turned = d * c_part - pltpu.roll(d, HEAD // 2, 1) * s_part
                ddelta[pl.ds(at, SUB), cols] = turned.astype(BF)

    def group(used, i):
        chunks = [*range(0, used, CHUNK), *range(n_prompt, n_keys, CHUNK)]
        x, y = (Unit(i * PAIR + u, u, used) for u in range(PAIR))
        for at in chunks:
            x.score(at)
        x.scored()
        for at in chunks:
            x.weigh(at)
            y.score(at)
        x.weighed()
        y.scored()
        for at in chunks:
            x.differ(at)
            y.weigh(at)
        y.weighed()
        for at in chunks:
            y.differ(at)
        x.finish()
        y.finish()

    for used in range(SPAN, n_prompt + 1, SPAN):

        @pl.when(jnp.logical_and(count > used - SPAN, count <= used))
        def _(used=used):
            def step(i, carry):
                group(used, i)
                return carry

            lax.fori_loop(0, (n_live + PAIR - 1) // PAIR, step, 0)

    for c in range(n_comp):
        down_ref[pl.ds(2 * c * tokens, tokens, 2), :] = own_dkeys[c] * inv_scale
        down_ref[pl.ds(2 * c * tokens + 1, tokens, 2), :] = own_dvalues[c]
    copies = [
        pltpu.make_async_copy(out_ref, out_hbm, sems.at[0]),
        pltpu.make_async_copy(down_ref, down_hbm, sems.at[1]),
    ]
    for copy in copies:
        copy.start()
    dprompt_ref[...] = jnp.zeros_like(dprompt_ref)
    for j in range(n_blocks):
        target = slots[prompt * n_blocks + j] // 2
        span = slice(j * tokens, (j + 1) * tokens)
        dprompt_ref[target, 0:tokens] = (dkeys[span] * inv_scale).astype(BF)
        dprompt_ref[target, tokens : 2 * tokens] = dvalues[span].astype(BF)
    grad_rows = dprompt_ref.shape[1] - 2 * tokens
    spans = (pl.ds(0, 2 * tokens), pl.ds(2 * tokens, grad_rows))
    for i, rows_of in enumerate(spans):
        copies.append(
            pltpu.make_async_copy(dprompt_ref.at[:, rows_of, :], dprompt_hbm.at[:, rows_of, :], sems.at[2 + i])
        )
    copies[2].start()
    dd = ddelta[...]
    dup = dot(mid[...].T, dd)
    pack_rows(dup, dup.shape[0] // dprompt_ref.shape[0], dprompt_ref, 2 * tokens)
    copies[3].start()
    split_halves(dot_nt(dd, up[...]), dmid_send, dmid_keep)
    for copy in copies:
        copy.wait()


def attend(prompts, counts, lengths, slots, mid_kept, mid_other, base, up, gathered, g_rows, own, cosine, sine):
    n_tokens, width = base.shape
    n_comp = lengths.shape[0]
    tokens = n_tokens // n_comp
    rank = up.shape[0]
    n_dp = gathered.shape[0]
    n_prompt = slots.shape[0] // counts.shape[0] * tokens
    n_keys = n_prompt + tokens
    rows = width // HEAD * SUB
    halves = (shape(mid_kept.shape, F32),) * 2
    grad_rows = rank // n_dp * width // HEAD
    return call(
        attention,
        (
            shape(base.shape, BF),
            *halves,
            shape((n_dp, 2 * tokens + grad_rows, HEAD), BF),
            shape((2 * n_tokens, HEAD), F32),
        ),
        [SM] * 4 + [VM] * 12,
        (HBM, VM, VM, HBM, HBM),
        56,
        [
            pltpu.SMEM((n_tokens // SUB,), jnp.int32),
            pltpu.VMEM((n_tokens, rank), BF),
            pltpu.VMEM((n_prompt, HEAD), BF),
            pltpu.VMEM((n_prompt, HEAD), BF),
            pltpu.VMEM((HEAD, n_prompt), BF),
            pltpu.VMEM((HEAD, n_prompt), BF),
            pltpu.VMEM((n_tokens // SUB, rows, HEAD), BF),
            pltpu.VMEM((PAIR, n_keys, rows), F32),
            pltpu.VMEM((PAIR, n_keys, rows), F32),
            pltpu.VMEM((PAIR, n_keys, rows), BF),
            pltpu.VMEM((PAIR, n_keys, rows), BF),
            pltpu.VMEM((n_prompt, HEAD), F32),
            pltpu.VMEM((n_prompt, HEAD), F32),
            pltpu.VMEM((n_comp, tokens, HEAD), F32),
            pltpu.VMEM((n_comp, tokens, HEAD), F32),
            pltpu.VMEM(base.shape, BF),
            pltpu.VMEM(base.shape, BF),
            pltpu.VMEM((n_dp, 2 * tokens + grad_rows, HEAD), BF),
            pltpu.VMEM((2 * n_tokens, HEAD), F32),
            pltpu.SemaphoreType.DMA((4,)),
        ],
    )(prompts, counts, lengths, slots, mid_kept, mid_other, base, up, gathered, g_rows, *own, cosine, sine)


def down_gradient(dmid_kept, dmid_other, hidden, out_ref, dmid):
    join_halves(dmid_kept, dmid_other, dmid)
    ddown = dot(dmid[...].T, hidden[...])
    pack_rows(ddown, ddown.shape[0] // out_ref.shape[0], out_ref, 0)


def finish_prompt(prompts, slots, got, dprompt_ref, dup_ref):
    n_dp = got.shape[0]
    rows = dprompt_ref.shape[0] // 4
    per_prompt = slots.shape[0] * 4 // prompts.shape[0]
    labels = stored_prompts(slots, lax.axis_index("dp"), per_prompt)
    for i in range(2):
        dk = jnp.zeros((rows, HEAD), F32)
        dv = jnp.zeros((rows, HEAD), F32)
        for e in range(n_dp):
            mine = prompts[e] == labels[i]
            dk += jnp.where(mine, got[e, 0:rows].astype(F32), 0.0)
            dv += jnp.where(mine, got[e, rows : 2 * rows].astype(F32), 0.0)
        dprompt_ref[pl.ds(2 * rows * i, rows, 2), :] = dk
        dprompt_ref[pl.ds(2 * rows * i + 1, rows, 2), :] = dv
    unpack_sum(got, dup_ref.shape[0], 2 * rows, dup_ref)


def finish_down(got, ddown_ref):
    unpack_sum(got, ddown_ref.shape[0], 0, ddown_ref)


def sum_over_tensor(send, keep, sent, beside=()):
    n = lax.axis_size("tensor")
    swap = [(i, i ^ 1) for i in range(n)]
    pair = (keep + lax.ppermute(send, "tensor", swap)).astype(sent)
    pair, beside = lax.optimization_barrier((pair, beside))
    total = pair.astype(F32)
    for k in range(2, n, 2):
        total += lax.ppermute(pair, "tensor", [(i, (i + k) % n) for i in range(n)]).astype(F32)
    kept = total.astype(BF)
    return kept, lax.ppermute(kept, "tensor", swap), beside


def local(
    hidden,
    base,
    own_kv,
    prompt_kv,
    down,
    up,
    grad,
    prompts,
    counts,
    lengths,
    slots,
):
    n_tokens, width = hidden.shape
    n_comp = lengths.shape[0]
    tokens = n_tokens // n_comp
    rank = down.shape[0]
    n_dp = lax.axis_size("dp")
    half_tokens = n_tokens // 2
    stored = prompt_kv.reshape(-1, HEAD)
    own = own_kv.reshape(-1, HEAD)

    halves = (shape((half_tokens, rank), F32),) * 2
    table = shape((tokens, HEAD), F32)
    mid_send, mid_keep, send, cosine, sine = call(
        prepare,
        (*halves, shape((n_dp, 2, tokens, HEAD), BF), table, table),
        [SM] * 3 + [VM] * 3,
        (VM,) * 5,
        56,
        [pltpu.VMEM(stored.shape, F32)],
    )(prompts, counts, slots, hidden, down, stored)
    gathered = lax.all_to_all(send, "dp", 0, 0)

    mid_kept, mid_other, (grad, own) = sum_over_tensor(mid_send, mid_keep, F32, (grad, own))
    rows = width // HEAD * SUB
    g_rows, *own = call(
        prepare_own,
        (
            shape((n_tokens // SUB, rows, HEAD), BF),
            *(shape((n_comp, tokens, HEAD), BF),) * 2,
            *(shape((n_comp, HEAD, tokens), BF),) * 2,
        ),
        [SM] + [VM] * 2,
        (VM,) * 5,
        56,
        [pltpu.VMEM(own.shape, F32)],
    )(lengths, grad, own)

    out, dmid_send, dmid_keep, dprompt, down_own = attend(
        prompts, counts, lengths, slots, mid_kept, mid_other, base, up, gathered, g_rows, own, cosine, sine
    )
    grad_rows = rank // n_dp * width // HEAD
    got = lax.all_to_all(dprompt, "dp", 0, 0)
    dmid_kept, dmid_other, _ = sum_over_tensor(dmid_send, dmid_keep, BF)
    ddown_parts = call(
        down_gradient,
        shape((n_dp, grad_rows, HEAD), BF),
        [VM] * 3,
        VM,
        6,
        [pltpu.VMEM((n_tokens, rank), BF)],
    )(dmid_kept, dmid_other, hidden)
    ddown_parts, got = lax.optimization_barrier((ddown_parts, got))
    grad_shape = shape((rank // n_dp, width), F32)
    dprompt, dup = call(
        finish_prompt,
        (shape(stored.shape, F32), grad_shape),
        [SM] * 2 + [VM],
        (VM,) * 2,
        6,
    )(prompts, slots, got)
    ddown = call(finish_down, grad_shape, [VM], VM, 4)(lax.all_to_all(ddown_parts, "dp", 0, 0))
    return (
        out,
        ddown,
        dup,
        dprompt.reshape(prompt_kv.shape),
        down_own.reshape(own_kv.shape),
    )


def solution(mesh):
    placed = (
        P("dp", "tensor"),
        P("dp", "tensor"),
        P("dp", None, "tensor", None),
        P("dp", None, "tensor", None),
        P(None, "tensor"),
        P(None, "tensor"),
        P("dp", "tensor"),
        P(),
        P(),
        P("dp"),
        P(),
    )
    return jax.shard_map(
        local,
        mesh=mesh,
        in_specs=placed,
        out_specs=(
            P("dp", "tensor"),
            P("dp", "tensor"),
            P("dp", "tensor"),
            P("dp", None, "tensor", None),
            P("dp", None, "tensor", None),
        ),
        check_vma=False,
    )
```

```python
import math

import jax
import jax.numpy as jnp
from jax import lax
from jax.experimental import pallas as pl
from jax.experimental.pallas import tpu as pltpu
from jax.sharding import PartitionSpec as P

ROPE_BASE = 1000000.0
BF = jnp.bfloat16
F32 = jnp.float32
HEAD = 128
SUB = 32
CHUNK = 128
PAIR = 2
SPAN = 256
MIB = 1024 * 1024
VM = pl.BlockSpec(memory_space=pltpu.VMEM)
SM = pl.BlockSpec(memory_space=pltpu.SMEM)
HBM = pl.BlockSpec(memory_space=pltpu.HBM)


def shape(dims, dtype):
    return jax.ShapeDtypeStruct(dims, dtype)


def dot(a, b):
    return jnp.dot(a, b, preferred_element_type=F32)


def dot_nt(a, b):
    return lax.dot_general(a, b, (((1,), (1,)), ((), ())), preferred_element_type=F32)


def call(body, out, in_specs, out_specs, mib, scratch=()):
    return pl.pallas_call(
        body,
        out_shape=out,
        in_specs=in_specs,
        out_specs=out_specs,
        scratch_shapes=list(scratch),
        compiler_params=pltpu.CompilerParams(vmem_limit_bytes=mib * MIB),
    )


def in_hbm(*arrays):
    return [pltpu.with_memory_space_constraint(x, pltpu.HBM) for x in arrays]


def in_vmem(*arrays):
    return [pltpu.with_memory_space_constraint(x, pltpu.VMEM) for x in arrays]


def stored_prompts(slots, me, per_prompt):
    first = jnp.int32(0)
    second = jnp.int32(0)
    for j in range(slots.shape[0]):
        slot = slots[j]
        first = jnp.where(slot == 2 * me, j // per_prompt, first)
        second = jnp.where(slot == 2 * me + 1, j // per_prompt, second)
    return first, second


def split_halves(value, send_ref, keep_ref):
    core = lax.rem(lax.axis_index("tensor"), 2)
    half = keep_ref.shape[0]
    send_ref[...] = jnp.where(core == 0, value[half:], value[:half])
    keep_ref[...] = jnp.where(core == 0, value[:half], value[half:])


def join_halves(kept, other, ref):
    core = lax.rem(lax.axis_index("tensor"), 2)
    half = kept.shape[0]
    ref[pl.ds(pl.multiple_of(core * half, half), half), :] = kept[...]
    ref[pl.ds(pl.multiple_of((1 - core) * half, half), half), :] = other[...]


def pack_rows(value, part, ref, first):
    for e in range(ref.shape[0]):
        rows = value[e * part : (e + 1) * part]
        for k in range(value.shape[1] // HEAD // 2):
            left = rows[:, 2 * k * HEAD : (2 * k + 1) * HEAD]
            right = rows[:, (2 * k + 1) * HEAD : (2 * k + 2) * HEAD]
            pair = jnp.concatenate([left, right], axis=0).astype(BF)
            ref[e, first + 2 * k * part : first + 2 * (k + 1) * part] = pair


def unpack_sum(got, part, first, out_ref):
    for k in range(out_ref.shape[1] // HEAD // 2):
        span = slice(first + 2 * k * part, first + 2 * (k + 1) * part)
        pair = got[0, span].astype(F32)
        for e in range(1, got.shape[0]):
            pair += got[e, span].astype(F32)
        out_ref[:, 2 * k * HEAD : (2 * k + 1) * HEAD] = pair[:part]
        out_ref[:, (2 * k + 1) * HEAD : (2 * k + 2) * HEAD] = pair[part:]


def prepare(prompts, counts, slots, hidden, down, stored, mid_send, mid_keep, send_ref, cosine, sine, wide):
    split_halves(dot_nt(hidden[...], down[...]), mid_send, mid_keep)
    n_dp = send_ref.shape[0]
    rows = send_ref.shape[2]
    wide[...] = stored[...].astype(F32)
    per_prompt = slots.shape[0] * 4 // prompts.shape[0]
    _, second = stored_prompts(slots, lax.axis_index("dp"), per_prompt)
    keys = wide[pl.ds(0, 2 * rows, 2), :].astype(BF)
    values = wide[pl.ds(1, 2 * rows, 2), :].astype(BF)
    for e in range(n_dp):
        take = prompts[e] == second
        send_ref[e, 0] = jnp.where(take, keys[rows:], keys[:rows])
        send_ref[e, 1] = jnp.where(take, values[rows:], values[:rows])
    lane = lax.broadcasted_iota(jnp.int32, cosine.shape, 1)
    token = lax.broadcasted_iota(jnp.int32, cosine.shape, 0)
    pair = lax.rem(lane, HEAD // 2).astype(F32)
    frequency = jnp.exp2(pair * (-2.0 / HEAD * math.log2(ROPE_BASE)))
    position = counts[prompts[lax.axis_index("dp")]] + token
    angles = position.astype(F32) * frequency
    cosine[...] = jnp.cos(angles)
    sin = jnp.sin(angles)
    sine[...] = jnp.where(lane < HEAD // 2, -sin, sin)


def prepare_own(
    lengths,
    grad,
    own,
    base_hbm,
    g_rows,
    own_keys,
    own_values,
    base,
    wide,
    sem,
):
    copy = pltpu.make_async_copy(base_hbm, base, sem)
    copy.start()
    n_comp, tokens, _ = own_keys.shape
    n_sub = tokens // SUB
    wide[...] = own[...].astype(F32)
    token_ids = lax.broadcasted_iota(jnp.int32, (tokens, HEAD), 0)
    for c in range(n_comp):
        k = wide[pl.ds(2 * c * tokens, tokens, 2), :].astype(BF)
        v = wide[pl.ds(2 * c * tokens + 1, tokens, 2), :].astype(BF)
        own_keys[c] = k
        own_values[c] = v
        live = token_ids < lengths[c]
        for h in range(grad.shape[1] // HEAD):
            g = grad[c * tokens : (c + 1) * tokens, h * HEAD : (h + 1) * HEAD].astype(F32)
            g = jnp.where(live, g, 0.0).astype(BF)
            for s in range(n_sub):
                g_rows[c * n_sub + s, h * SUB : (h + 1) * SUB] = g[s * SUB : (s + 1) * SUB]
    copy.wait()


def attention(
    prompts,
    counts,
    lengths,
    slots,
    mid_kept,
    mid_other,
    base,
    up_hbm,
    gathered,
    g_rows,
    own_keys_hbm,
    own_values_hbm,
    cosine_hbm,
    sine_hbm,
    out_hbm,
    dmid_send,
    dmid_keep,
    dprompt_hbm,
    down_hbm,
    units,
    up,
    own_keys,
    own_values,
    cosine,
    sine,
    own_keys_t,
    own_values_t,
    mid,
    keys,
    values,
    keys_t,
    values_t,
    q_rows,
    scores,
    dprobs,
    probs_low,
    dscores,
    dkeys,
    dvalues,
    own_dkeys,
    own_dvalues,
    ddelta,
    out_ref,
    dprompt_ref,
    down_ref,
    dup_ref,
    zeros,
    sems,
    in_sems,
):
    n_comp = lengths.shape[0]
    tokens = base.shape[0] // n_comp
    heads = base.shape[1] // HEAD
    n_sub = tokens // SUB
    rows = heads * SUB
    n_prompt = keys.shape[0]
    n_keys = n_prompt + tokens
    n_blocks = n_prompt // tokens
    prompt = prompts[lax.axis_index("dp")]
    count = counts[prompt]
    pairs = (
        (up_hbm, up),
        (own_keys_hbm, own_keys),
        (own_values_hbm, own_values),
        (cosine_hbm, cosine),
        (sine_hbm, sine),
    )
    copies_in = [pltpu.make_async_copy(a, b, in_sems.at[i]) for i, (a, b) in enumerate(pairs)]
    for copy in copies_in:
        copy.start()
    join_halves(mid_kept, mid_other, mid)
    inv_scale = 1.0 / math.sqrt(HEAD)
    exp2_scale = inv_scale * math.log2(math.e)

    dkeys[...] = jnp.zeros_like(dkeys)
    dvalues[...] = jnp.zeros_like(dvalues)
    own_dkeys[...] = jnp.zeros_like(own_dkeys)
    own_dvalues[...] = jnp.zeros_like(own_dvalues)
    zeros[...] = jnp.zeros_like(zeros)
    for j in range(n_blocks):
        source = slots[prompt * n_blocks + j] // 2
        span = slice(j * tokens, (j + 1) * tokens)
        k = gathered[source, 0]
        v = gathered[source, 1]
        keys[span] = k
        values[span] = v
        keys_t[:, span] = k.T
        values_t[:, span] = v.T
    for copy in copies_in:
        copy.wait()
    for c in range(n_comp):
        own_keys_t[c] = own_keys[c].T
        own_values_t[c] = own_values[c].T
    cos = cosine[...]
    sin = sine[...]

    n_live = jnp.int32(0)
    for c in range(n_comp):
        n_live += (lengths[c] + SUB - 1) // SUB
    at_live = jnp.int32(0)
    at_dead = n_live
    for c in range(n_comp):
        for s in range(n_sub):
            live = s * SUB < lengths[c]
            place = jnp.where(live, at_live, at_dead)
            units[place] = c * n_sub + s
            at_live += jnp.where(live, 1, 0)
            at_dead += jnp.where(live, 0, 1)

    for c in range(n_comp):
        span = slice(c * tokens, (c + 1) * tokens)
        delta = dot(mid[span], up[...])
        for h in range(heads):
            cols = slice(h * HEAD, (h + 1) * HEAD)
            d = delta[:, cols]
            turned = d * cos + pltpu.roll(d, HEAD // 2, 1) * sin
            q = (base[span, cols].astype(F32) + turned).astype(BF)
            for s in range(n_sub):
                q_rows[c * n_sub + s, h * SUB : (h + 1) * SUB] = q[s * SUB : (s + 1) * SUB]

    for n in range(n_comp * n_sub):

        @pl.when(n >= n_live)
        def _(n=n):
            span = pl.ds(pl.multiple_of(units[n] * SUB, SUB), SUB)
            pltpu.make_async_copy(zeros, out_hbm.at[span], sems.at[0]).start()
            ddelta[span] = zeros[...]

    class Unit:
        def __init__(self, n, u, used):
            self.u = u
            self.used = used
            unit = units[n]
            self.c = unit // n_sub
            self.first = (unit % n_sub) * SUB
            self.q = q_rows[unit]
            self.g = g_rows[unit]
            self.q_t = self.q.T
            self.g_t = self.g.T
            self.top = None
            self.total = jnp.zeros((8, rows), F32)
            self.mean = jnp.zeros((8, rows), F32)

        def score(self, at, size):
            span = slice(at, at + size)
            key_token = lax.broadcasted_iota(jnp.int32, (size, rows), 0)
            if at < self.used:
                x = dot(keys[span], self.q_t)
                allowed = key_token < count - at if at + size > self.used - SPAN else None
            else:
                x = dot(own_keys[self.c, at - n_prompt : at - n_prompt + size], self.q_t)
                col_token = self.first + lax.broadcasted_iota(jnp.int32, (size, rows), 1) % SUB
                allowed = key_token + (at - n_prompt) <= col_token
            if allowed is not None:
                x = jnp.where(allowed, x, -1e30)
            scores[self.u, span] = x
            t = jnp.max(x.reshape(size // 8, 8, rows), axis=0)
            self.top = t if self.top is None else jnp.maximum(self.top, t)

        def scored(self):
            self.top = jnp.max(self.top, axis=0, keepdims=True)

        def weigh(self, at, size):
            span = slice(at, at + size)
            if at < n_prompt:
                dp = dot(values[span], self.g_t)
            else:
                dp = dot(own_values[self.c, at - n_prompt : at - n_prompt + size], self.g_t)
            w = jnp.exp2((scores[self.u, span] - self.top) * exp2_scale)
            scores[self.u, span] = w
            dprobs[self.u, span] = dp
            self.total += jnp.sum(w.reshape(size // 8, 8, rows), axis=0)
            self.mean += jnp.sum((w * dp).reshape(size // 8, 8, rows), axis=0)

        def weighed(self):
            self.inv = 1.0 / jnp.sum(self.total, axis=0, keepdims=True)
            self.mean = jnp.sum(self.mean, axis=0, keepdims=True) * self.inv

        def differ(self, at, size):
            span = slice(at, at + size)
            p = scores[self.u, span] * self.inv
            probs_low[self.u, span] = p.astype(BF)
            dscores[self.u, span] = (p * (dprobs[self.u, span] - self.mean)).astype(BF)

        def finish(self):
            u, c = self.u, self.c
            used = self.used
            low = probs_low[u, :used]
            ds = dscores[u, :used]
            own_low = probs_low[u, n_prompt:]
            own_ds = dscores[u, n_prompt:]
            out = (dot(values_t[:, :used], low) + dot(own_values_t[c], own_low)).T
            dq = ((dot(keys_t[:, :used], ds) + dot(own_keys_t[c], own_ds)) * inv_scale).T
            dvalues[:used] += dot(low, self.g)
            dkeys[:used] += dot(ds, self.q)
            own_dvalues[c] += dot(own_low, self.g)
            own_dkeys[c] += dot(own_ds, self.q)
            first = self.first
            at = pl.multiple_of(c * tokens + first, SUB)
            row_live = lax.broadcasted_iota(jnp.int32, (SUB, HEAD), 0) + first < lengths[c]
            c_part = cosine[pl.ds(first, SUB), :]
            s_part = sine[pl.ds(first, SUB), :]
            for h in range(heads):
                cols = slice(h * HEAD, (h + 1) * HEAD)
                o = out[h * SUB : (h + 1) * SUB]
                out_ref[pl.ds(at, SUB), cols] = jnp.where(row_live, o, 0.0).astype(BF)
                d = dq[h * SUB : (h + 1) * SUB]
                turned = d * c_part - pltpu.roll(d, HEAD // 2, 1) * s_part
                ddelta[pl.ds(at, SUB), cols] = turned.astype(BF)
            span = pl.ds(at, SUB)
            pltpu.make_async_copy(out_ref.at[span], out_hbm.at[span], sems.at[0]).start()

    def group(used, i):
        chunks = [(at, min(CHUNK, used - at)) for at in range(0, used, CHUNK)] + [(n_prompt, tokens)]
        x, y = (Unit(i * PAIR + u, u, used) for u in range(PAIR))
        for at, size in chunks:
            x.score(at, size)
        x.scored()
        for at, size in chunks:
            x.weigh(at, size)
            y.score(at, size)
        x.weighed()
        y.scored()
        for at, size in chunks:
            x.differ(at, size)
            y.weigh(at, size)
        y.weighed()
        for at, size in chunks:
            y.differ(at, size)
        x.finish()
        y.finish()

    def alone(used, n):
        chunks = [(at, min(CHUNK, used - at)) for at in range(0, used, CHUNK)] + [(n_prompt, tokens)]
        x = Unit(n, 0, used)
        for at, size in chunks:
            x.score(at, size)
        x.scored()
        for at, size in chunks:
            x.weigh(at, size)
        x.weighed()
        for at, size in chunks:
            x.differ(at, size)
        x.finish()

    for used in range(SPAN, n_prompt + 1, SPAN):

        @pl.when(jnp.logical_and(count > used - SPAN, count <= used))
        def _(used=used):
            def step(i, carry):
                group(used, i)
                return carry

            lax.fori_loop(0, n_live // PAIR, step, 0)

            @pl.when(n_live % PAIR == 1)
            def _():
                alone(used, n_live - 1)

    copies = []
    for j in range(n_blocks):
        target = slots[prompt * n_blocks + j] // 2
        span = slice(j * tokens, (j + 1) * tokens)
        dprompt_ref[j, 0:tokens] = (dkeys[span] * inv_scale).astype(BF)
        dprompt_ref[j, tokens : 2 * tokens] = dvalues[span].astype(BF)
        block = dprompt_hbm.at[target, pl.ds(0, 2 * tokens)]
        copies.append(pltpu.make_async_copy(dprompt_ref.at[j], block, sems.at[3 + j]))
        copies[-1].start()
    for c in range(n_comp):
        down_ref[pl.ds(2 * c * tokens, tokens, 2), :] = own_dkeys[c] * inv_scale
        down_ref[pl.ds(2 * c * tokens + 1, tokens, 2), :] = own_dvalues[c]
    copies.append(pltpu.make_async_copy(down_ref, down_hbm, sems.at[2]))
    copies[-1].start()
    dd = ddelta[...]
    dup = dot(mid[...].T, dd)
    pack_rows(dup, dup.shape[0] // dup_ref.shape[0], dup_ref, 0)
    rest = dprompt_hbm.at[:, pl.ds(2 * tokens, dup_ref.shape[1])]
    copies.append(pltpu.make_async_copy(dup_ref, rest, sems.at[1]))
    copies[-1].start()
    split_halves(dot_nt(dd, up[...]), dmid_send, dmid_keep)
    for copy in copies:
        copy.wait()
    pltpu.make_async_copy(out_ref, out_hbm, sems.at[0]).wait()


def attend(prompts, counts, lengths, slots, mid_kept, mid_other, base, up, gathered, g_rows, own, cosine, sine):
    n_tokens, width = base.shape
    n_comp = lengths.shape[0]
    tokens = n_tokens // n_comp
    rank = mid_kept.shape[1]
    n_dp = gathered.shape[0]
    grad_rows = rank // n_dp * width // HEAD
    n_prompt = slots.shape[0] // counts.shape[0] * tokens
    n_keys = n_prompt + tokens
    rows = width // HEAD * SUB
    prompts, counts, lengths, slots = in_hbm(prompts, counts, lengths, slots)
    g_rows, base = in_vmem(g_rows, base)
    up, *own, cosine, sine = in_hbm(up, *own, cosine, sine)
    return call(
        attention,
        (
            pltpu.HBM(base.shape, BF),
            *(pltpu.VMEM(mid_kept.shape, F32),) * 2,
            pltpu.HBM((n_dp, 2 * tokens + grad_rows, HEAD), BF),
            pltpu.HBM((2 * n_tokens, HEAD), F32),
        ),
        [SM] * 4 + [VM] * 3 + [HBM] + [VM] * 2 + [HBM] * 4,
        (HBM, VM, VM, HBM, HBM),
        44,
        [
            pltpu.SMEM((n_tokens // SUB,), jnp.int32),
            pltpu.VMEM(up.shape, BF),
            *(pltpu.VMEM(part.shape, BF) for part in own),
            pltpu.VMEM(cosine.shape, F32),
            pltpu.VMEM(sine.shape, F32),
            pltpu.VMEM((n_comp, HEAD, tokens), BF),
            pltpu.VMEM((n_comp, HEAD, tokens), BF),
            pltpu.VMEM((n_tokens, rank), BF),
            pltpu.VMEM((n_prompt, HEAD), BF),
            pltpu.VMEM((n_prompt, HEAD), BF),
            pltpu.VMEM((HEAD, n_prompt), BF),
            pltpu.VMEM((HEAD, n_prompt), BF),
            pltpu.VMEM((n_tokens // SUB, rows, HEAD), BF),
            pltpu.VMEM((PAIR, n_keys, rows), F32),
            pltpu.VMEM((PAIR, n_keys, rows), F32),
            pltpu.VMEM((PAIR, n_keys, rows), BF),
            pltpu.VMEM((PAIR, n_keys, rows), BF),
            pltpu.VMEM((n_prompt, HEAD), F32),
            pltpu.VMEM((n_prompt, HEAD), F32),
            pltpu.VMEM((n_comp, tokens, HEAD), F32),
            pltpu.VMEM((n_comp, tokens, HEAD), F32),
            pltpu.VMEM(base.shape, BF),
            pltpu.VMEM(base.shape, BF),
            pltpu.VMEM((n_prompt // tokens, 2 * tokens, HEAD), BF),
            pltpu.VMEM((2 * n_tokens, HEAD), F32),
            pltpu.VMEM((n_dp, grad_rows, HEAD), BF),
            pltpu.VMEM((SUB, width), BF),
            pltpu.SemaphoreType.DMA((3 + n_prompt // tokens,)),
            pltpu.SemaphoreType.DMA((5,)),
        ],
    )(prompts, counts, lengths, slots, mid_kept, mid_other, base, up, gathered, g_rows, *own, cosine, sine)


def down_gradient(dmid_kept, dmid_other, hidden, *refs):
    *out_refs, dmid, ddown = refs
    join_halves(dmid_kept, dmid_other, dmid)
    ddown[...] = dot(dmid[...].T, hidden[...])
    side = len(out_refs)
    part = ddown.shape[0] // side**2
    x = lax.rem(lax.axis_index("dp"), side)
    for k, out_ref in enumerate(out_refs):
        for y in range(side):
            owner = y * side + lax.rem(x + k, side)
            rows = ddown[pl.ds(pl.multiple_of(owner * part, part), part), :]
            pack_rows(rows, part, out_ref.at[pl.ds(y, 1)], 0)


def sum_along_x(*refs):
    side = len(refs) // 2
    got, out_refs = refs[:side], refs[side:]
    y = lax.div(lax.axis_index("dp"), side)
    for k, out_ref in enumerate(out_refs):
        row = lax.rem(y + k, side)
        total = got[0][row].astype(F32)
        for ref in got[1:]:
            total += ref[row].astype(F32)
        out_ref[...] = total.astype(BF)


def finish_down(*refs):
    *got, ddown_ref = refs
    part = ddown_ref.shape[0]
    total = got[0][...].astype(F32)
    for ref in got[1:]:
        total += ref[...].astype(F32)
    for k in range(ddown_ref.shape[1] // HEAD):
        ddown_ref[:, k * HEAD : (k + 1) * HEAD] = total[k * part : (k + 1) * part]


def finish_prompt(prompts, slots, got, dprompt_ref, dup_ref):
    n_dp = got.shape[0]
    rows = dprompt_ref.shape[0] // 4
    per_prompt = slots.shape[0] * 4 // prompts.shape[0]
    labels = stored_prompts(slots, lax.axis_index("dp"), per_prompt)
    for i in range(2):
        dk = jnp.zeros((rows, HEAD), F32)
        dv = jnp.zeros((rows, HEAD), F32)
        for e in range(n_dp):
            mine = prompts[e] == labels[i]
            dk += jnp.where(mine, got[e, 0:rows].astype(F32), 0.0)
            dv += jnp.where(mine, got[e, rows : 2 * rows].astype(F32), 0.0)
        dprompt_ref[pl.ds(2 * rows * i, rows, 2), :] = dk
        dprompt_ref[pl.ds(2 * rows * i + 1, rows, 2), :] = dv
    unpack_sum(got, dup_ref.shape[0], 2 * rows, dup_ref)


def along_x(side, k):
    return [(side * y + x, side * y + (x + k) % side) for y in range(side) for x in range(side)]


def along_y(side, k):
    return [(side * y + x, side * ((y + k) % side) + x) for y in range(side) for x in range(side)]


def sum_over_tensor(send, keep, sent, beside=None):
    n = lax.axis_size("tensor")
    swap = [(i, i ^ 1) for i in range(n)]
    pair = (keep + lax.ppermute(send, "tensor", swap)).astype(sent)
    got = [lax.ppermute(pair, "tensor", [(i, (i + k) % n) for i in range(n)]) for k in range(2, n, 2)]
    done = None
    if beside is not None:
        got, done = lax.optimization_barrier((got, beside(pair)))
    total = pair.astype(F32)
    for part in got:
        total += part.astype(F32)
    kept = total.astype(BF)
    return kept, lax.ppermute(kept, "tensor", swap), done


def local(
    hidden,
    base,
    own_kv,
    prompt_kv,
    down,
    up,
    grad,
    prompts,
    counts,
    lengths,
    slots,
):
    n_tokens, width = hidden.shape
    n_comp = lengths.shape[0]
    tokens = n_tokens // n_comp
    rank = down.shape[0]
    n_dp = lax.axis_size("dp")
    half_tokens = n_tokens // 2
    stored = prompt_kv.reshape(-1, HEAD)
    own = own_kv.reshape(-1, HEAD)

    mid_send, mid_keep, send, cosine, sine = call(
        prepare,
        (
            *(pltpu.VMEM((half_tokens, rank), F32),) * 2,
            pltpu.HBM((n_dp, 2, tokens, HEAD), BF),
            *(pltpu.HBM((tokens, HEAD), F32),) * 2,
        ),
        [SM] * 3 + [VM] * 3,
        (VM,) * 5,
        12,
        [pltpu.VMEM(stored.shape, F32)],
    )(*in_hbm(prompts, counts, slots, hidden, down, stored))
    gathered = lax.all_to_all(send, "dp", 0, 0)

    rows = width // HEAD * SUB

    def beside(pair):
        after, _ = lax.optimization_barrier(((grad, own), pair))
        return call(
            prepare_own,
            (
                pltpu.VMEM((n_tokens // SUB, rows, HEAD), BF),
                *(pltpu.HBM((n_comp, tokens, HEAD), BF),) * 2,
                pltpu.VMEM(base.shape, BF),
            ),
            [SM] + [VM] * 2 + [HBM],
            (VM,) * 4,
            12,
            [pltpu.VMEM(own.shape, F32), pltpu.SemaphoreType.DMA],
        )(*in_hbm(lengths, *after, base))

    mid_kept, mid_other, (g_rows, *own_parts, base) = sum_over_tensor(mid_send, mid_keep, F32, beside)
    out, dmid_send, dmid_keep, dprompt, down_own = attend(
        prompts, counts, lengths, slots, mid_kept, mid_other, base, up, gathered, g_rows, own_parts, cosine, sine
    )
    grad_rows = rank // n_dp * width // HEAD
    got = lax.all_to_all(dprompt, "dp", 0, 0)
    dmid_kept, dmid_other, _ = sum_over_tensor(dmid_send, dmid_keep, BF)
    grad_shape = shape((rank // n_dp, width), F32)
    side = math.isqrt(n_dp)
    pieces = call(
        down_gradient,
        (shape((side, grad_rows, HEAD), BF),) * side,
        [VM] * 3,
        (VM,) * side,
        8,
        [pltpu.VMEM((n_tokens, rank), BF), pltpu.VMEM((rank, width), F32)],
    )(dmid_kept, dmid_other, hidden)
    pieces = [pieces[0], *(lax.ppermute(pieces[k], "dp", along_x(side, k)) for k in range(1, side))]
    pieces = call(sum_along_x, (shape((grad_rows, HEAD), BF),) * side, [VM] * side, (VM,) * side, 4)(*pieces)
    pieces = [pieces[0], *(lax.ppermute(pieces[k], "dp", along_y(side, k)) for k in range(1, side))]
    dprompt, dup = call(
        finish_prompt,
        (shape(stored.shape, F32), grad_shape),
        [SM] * 2 + [VM],
        (VM,) * 2,
        6,
    )(prompts, slots, got)
    pieces, dprompt, dup = lax.optimization_barrier((pieces, dprompt, dup))
    ddown = call(finish_down, grad_shape, [VM] * side, VM, 4)(*pieces)
    return (
        out,
        ddown,
        dup,
        dprompt.reshape(prompt_kv.shape),
        down_own.reshape(own_kv.shape),
    )


def solution(mesh):
    placed = (
        P("dp", "tensor"),
        P("dp", "tensor"),
        P("dp", None, "tensor", None),
        P("dp", None, "tensor", None),
        P(None, "tensor"),
        P(None, "tensor"),
        P("dp", "tensor"),
        P(),
        P(),
        P("dp"),
        P(),
    )
    return jax.shard_map(
        local,
        mesh=mesh,
        in_specs=placed,
        out_specs=(
            P("dp", "tensor"),
            P("dp", "tensor"),
            P("dp", "tensor"),
            P("dp", None, "tensor", None),
            P("dp", None, "tensor", None),
        ),
        check_vma=False,
    )
```

```python
import math

import jax
import jax.numpy as jnp
from jax import lax
from jax.experimental import pallas as pl
from jax.experimental.pallas import tpu as pltpu
from jax.sharding import PartitionSpec as P

ROPE_BASE = 1000000.0
BF = jnp.bfloat16
F32 = jnp.float32
HEAD = 128
SUB = 32
CHUNK = 128
PAIR = 2
SPAN = 256
MIB = 1024 * 1024
VM = pl.BlockSpec(memory_space=pltpu.VMEM)
SM = pl.BlockSpec(memory_space=pltpu.SMEM)
HBM = pl.BlockSpec(memory_space=pltpu.HBM)


def shape(dims, dtype):
    return jax.ShapeDtypeStruct(dims, dtype)


def dot(a, b):
    return jnp.dot(a, b, preferred_element_type=F32)


def dot_nt(a, b):
    return lax.dot_general(a, b, (((1,), (1,)), ((), ())), preferred_element_type=F32)


def call(body, out, in_specs, out_specs, mib, scratch=()):
    return pl.pallas_call(
        body,
        out_shape=out,
        in_specs=in_specs,
        out_specs=out_specs,
        scratch_shapes=list(scratch),
        compiler_params=pltpu.CompilerParams(vmem_limit_bytes=mib * MIB),
    )


def in_hbm(*arrays):
    return [pltpu.with_memory_space_constraint(x, pltpu.HBM) for x in arrays]


def in_vmem(*arrays):
    return [pltpu.with_memory_space_constraint(x, pltpu.VMEM) for x in arrays]


def stored_prompts(slots, me, per_prompt):
    first = jnp.int32(0)
    second = jnp.int32(0)
    for j in range(slots.shape[0]):
        slot = slots[j]
        first = jnp.where(slot == 2 * me, j // per_prompt, first)
        second = jnp.where(slot == 2 * me + 1, j // per_prompt, second)
    return first, second


def split_halves(value, send_ref, keep_ref):
    core = lax.rem(lax.axis_index("tensor"), 2)
    half = keep_ref.shape[0]
    send_ref[...] = jnp.where(core == 0, value[half:], value[:half])
    keep_ref[...] = jnp.where(core == 0, value[:half], value[half:])


def join_halves(kept, other, ref):
    core = lax.rem(lax.axis_index("tensor"), 2)
    half = kept.shape[0]
    ref[pl.ds(pl.multiple_of(core * half, half), half), :] = kept[...]
    ref[pl.ds(pl.multiple_of((1 - core) * half, half), half), :] = other[...]


def pack_rows(value, part, ref, first):
    for e in range(ref.shape[0]):
        rows = value[e * part : (e + 1) * part]
        for k in range(value.shape[1] // HEAD // 2):
            left = rows[:, 2 * k * HEAD : (2 * k + 1) * HEAD]
            right = rows[:, (2 * k + 1) * HEAD : (2 * k + 2) * HEAD]
            pair = jnp.concatenate([left, right], axis=0).astype(BF)
            ref[e, first + 2 * k * part : first + 2 * (k + 1) * part] = pair


def unpack_sum(got, part, first, out_ref):
    for k in range(out_ref.shape[1] // HEAD // 2):
        span = slice(first + 2 * k * part, first + 2 * (k + 1) * part)
        pair = got[0, span].astype(F32)
        for e in range(1, got.shape[0]):
            pair += got[e, span].astype(F32)
        out_ref[:, 2 * k * HEAD : (2 * k + 1) * HEAD] = pair[:part]
        out_ref[:, (2 * k + 1) * HEAD : (2 * k + 2) * HEAD] = pair[part:]


def prepare(
    prompts,
    slots,
    hidden_hbm,
    down_hbm,
    stored_hbm,
    mid_send,
    mid_keep,
    send_hbm,
    hidden,
    down,
    stored,
    wide,
    send,
    sems,
):
    n_dp, _, rows, _ = send.shape
    pairs = ((stored_hbm, stored), (down_hbm, down), (hidden_hbm, hidden))
    copies = [pltpu.make_async_copy(a, b, sems.at[i]) for i, (a, b) in enumerate(pairs)]
    for copy in copies:
        copy.start()
    per_prompt = slots.shape[0] * 4 // prompts.shape[0]
    _, second = stored_prompts(slots, lax.axis_index("dp"), per_prompt)
    copies[0].wait()
    wide[...] = stored[...].astype(F32)
    keys = wide[pl.ds(0, 2 * rows, 2), :].astype(BF)
    values = wide[pl.ds(1, 2 * rows, 2), :].astype(BF)
    for e in range(n_dp):
        take = prompts[e] == second
        send[e, 0] = jnp.where(take, keys[rows:], keys[:rows])
        send[e, 1] = jnp.where(take, values[rows:], values[:rows])
    sent = pltpu.make_async_copy(send, send_hbm, sems.at[3])
    sent.start()
    copies[1].wait()
    copies[2].wait()
    split_halves(dot_nt(hidden[...], down[...]), mid_send, mid_keep)
    sent.wait()


def rotary_tables(position, cosine, sine):
    lane = lax.broadcasted_iota(jnp.int32, cosine.shape, 1)
    token = lax.broadcasted_iota(jnp.int32, cosine.shape, 0)
    pair = lax.rem(lane, HEAD // 2).astype(F32)
    frequency = jnp.exp2(pair * (-2.0 / HEAD * math.log2(ROPE_BASE)))
    angles = (position + token).astype(F32) * frequency
    cosine[...] = jnp.cos(angles)
    sin = jnp.sin(angles)
    sine[...] = jnp.where(lane < HEAD // 2, -sin, sin)


def prepare_own(
    prompts,
    counts,
    lengths,
    grad,
    own,
    base_hbm,
    g_rows,
    own_keys,
    own_values,
    base,
    cosine,
    sine,
    wide,
    sem,
):
    copy = pltpu.make_async_copy(base_hbm, base, sem)
    copy.start()
    rotary_tables(counts[prompts[lax.axis_index("dp")]], cosine, sine)
    n_comp, tokens, _ = own_keys.shape
    n_sub = tokens // SUB
    wide[...] = own[...].astype(F32)
    token_ids = lax.broadcasted_iota(jnp.int32, (tokens, HEAD), 0)
    for c in range(n_comp):
        k = wide[pl.ds(2 * c * tokens, tokens, 2), :].astype(BF)
        v = wide[pl.ds(2 * c * tokens + 1, tokens, 2), :].astype(BF)
        own_keys[c] = k
        own_values[c] = v
        live = token_ids < lengths[c]
        for h in range(grad.shape[1] // HEAD):
            g = grad[c * tokens : (c + 1) * tokens, h * HEAD : (h + 1) * HEAD].astype(F32)
            g = jnp.where(live, g, 0.0).astype(BF)
            for s in range(n_sub):
                g_rows[c * n_sub + s, h * SUB : (h + 1) * SUB] = g[s * SUB : (s + 1) * SUB]
    copy.wait()


def attention(
    prompts,
    counts,
    lengths,
    slots,
    mid_kept,
    mid_other,
    base,
    up_hbm,
    gathered,
    g_rows,
    own_keys_hbm,
    own_values_hbm,
    cosine_hbm,
    sine_hbm,
    out_hbm,
    dmid_send,
    dmid_keep,
    dprompt_hbm,
    down_hbm,
    units,
    up,
    own_keys,
    own_values,
    cosine,
    sine,
    own_keys_t,
    own_values_t,
    mid,
    keys,
    values,
    keys_t,
    values_t,
    q_rows,
    scores,
    dprobs,
    probs_low,
    dscores,
    dkeys,
    dvalues,
    own_dkeys,
    own_dvalues,
    ddelta,
    out_ref,
    dprompt_ref,
    down_ref,
    dup_ref,
    zeros,
    sems,
    in_sems,
):
    n_comp = lengths.shape[0]
    tokens = base.shape[0] // n_comp
    heads = base.shape[1] // HEAD
    n_sub = tokens // SUB
    rows = heads * SUB
    n_prompt = keys.shape[0]
    n_keys = n_prompt + tokens
    n_blocks = n_prompt // tokens
    prompt = prompts[lax.axis_index("dp")]
    count = counts[prompt]
    pairs = (
        (up_hbm, up),
        (own_keys_hbm, own_keys),
        (own_values_hbm, own_values),
        (cosine_hbm, cosine),
        (sine_hbm, sine),
    )
    copies_in = [pltpu.make_async_copy(a, b, in_sems.at[i]) for i, (a, b) in enumerate(pairs)]
    for copy in copies_in:
        copy.start()
    join_halves(mid_kept, mid_other, mid)
    inv_scale = 1.0 / math.sqrt(HEAD)
    exp2_scale = inv_scale * math.log2(math.e)

    dkeys[...] = jnp.zeros_like(dkeys)
    dvalues[...] = jnp.zeros_like(dvalues)
    own_dkeys[...] = jnp.zeros_like(own_dkeys)
    own_dvalues[...] = jnp.zeros_like(own_dvalues)
    zeros[...] = jnp.zeros_like(zeros)
    for j in range(n_blocks):
        source = slots[prompt * n_blocks + j] // 2
        span = slice(j * tokens, (j + 1) * tokens)
        k = gathered[source, 0]
        v = gathered[source, 1]
        keys[span] = k
        values[span] = v
        keys_t[:, span] = k.T
        values_t[:, span] = v.T
    for copy in copies_in:
        copy.wait()
    for c in range(n_comp):
        own_keys_t[c] = own_keys[c].T
        own_values_t[c] = own_values[c].T
    cos = cosine[...]
    sin = sine[...]

    n_live = jnp.int32(0)
    for c in range(n_comp):
        n_live += (lengths[c] + SUB - 1) // SUB
    at_live = jnp.int32(0)
    at_dead = n_live
    for c in range(n_comp):
        for s in range(n_sub):
            live = s * SUB < lengths[c]
            place = jnp.where(live, at_live, at_dead)
            units[place] = c * n_sub + s
            at_live += jnp.where(live, 1, 0)
            at_dead += jnp.where(live, 0, 1)

    for c in range(n_comp):
        span = slice(c * tokens, (c + 1) * tokens)
        delta = dot(mid[span], up[...])
        for h in range(heads):
            cols = slice(h * HEAD, (h + 1) * HEAD)
            d = delta[:, cols]
            turned = d * cos + pltpu.roll(d, HEAD // 2, 1) * sin
            q = (base[span, cols].astype(F32) + turned).astype(BF)
            for s in range(n_sub):
                q_rows[c * n_sub + s, h * SUB : (h + 1) * SUB] = q[s * SUB : (s + 1) * SUB]

    for n in range(n_comp * n_sub):

        @pl.when(n >= n_live)
        def _(n=n):
            span = pl.ds(pl.multiple_of(units[n] * SUB, SUB), SUB)
            pltpu.make_async_copy(zeros, out_hbm.at[span], sems.at[0]).start()
            ddelta[span] = zeros[...]

    class Unit:
        def __init__(self, n, u, used):
            self.u = u
            self.used = used
            unit = units[n]
            self.c = unit // n_sub
            self.first = (unit % n_sub) * SUB
            self.q = q_rows[unit]
            self.g = g_rows[unit]
            self.q_t = self.q.T
            self.g_t = self.g.T
            self.top = None
            self.total = jnp.zeros((8, rows), F32)
            self.mean = jnp.zeros((8, rows), F32)

        def score(self, at, size):
            span = slice(at, at + size)
            key_token = lax.broadcasted_iota(jnp.int32, (size, rows), 0)
            if at < self.used:
                x = dot(keys[span], self.q_t)
                allowed = key_token < count - at if at + size > self.used - SPAN else None
            else:
                x = dot(own_keys[self.c, at - n_prompt : at - n_prompt + size], self.q_t)
                col_token = self.first + lax.broadcasted_iota(jnp.int32, (size, rows), 1) % SUB
                allowed = key_token + (at - n_prompt) <= col_token
            if allowed is not None:
                x = jnp.where(allowed, x, -1e30)
            scores[self.u, span] = x
            t = jnp.max(x.reshape(size // 8, 8, rows), axis=0)
            self.top = t if self.top is None else jnp.maximum(self.top, t)

        def scored(self):
            self.top = jnp.max(self.top, axis=0, keepdims=True)

        def weigh(self, at, size):
            span = slice(at, at + size)
            if at < n_prompt:
                dp = dot(values[span], self.g_t)
            else:
                dp = dot(own_values[self.c, at - n_prompt : at - n_prompt + size], self.g_t)
            w = jnp.exp2((scores[self.u, span] - self.top) * exp2_scale)
            scores[self.u, span] = w
            probs_low[self.u, span] = w.astype(BF)
            dprobs[self.u, span] = dp
            self.total += jnp.sum(w.reshape(size // 8, 8, rows), axis=0)
            self.mean += jnp.sum((w * dp).reshape(size // 8, 8, rows), axis=0)

        def weighed(self):
            self.inv = 1.0 / jnp.sum(self.total, axis=0, keepdims=True)
            self.mean = jnp.sum(self.mean, axis=0, keepdims=True) * self.inv

        def differ(self, at, size):
            span = slice(at, at + size)
            w = scores[self.u, span]
            dscores[self.u, span] = (w * (dprobs[self.u, span] - self.mean)).astype(BF)

        def finish(self):
            u, c = self.u, self.c
            used = self.used
            low = probs_low[u, :used]
            ds = dscores[u, :used]
            own_low = probs_low[u, n_prompt:]
            own_ds = dscores[u, n_prompt:]
            out = ((dot(values_t[:, :used], low) + dot(own_values_t[c], own_low)) * self.inv).T
            dq = ((dot(keys_t[:, :used], ds) + dot(own_keys_t[c], own_ds)) * (self.inv * inv_scale)).T
            column = jnp.broadcast_to(self.inv, (8, rows)).T[:, :1]
            q = (self.q.astype(F32) * column).astype(BF)
            g = (self.g.astype(F32) * column).astype(BF)
            dvalues[:used] += dot(low, g)
            dkeys[:used] += dot(ds, q)
            own_dvalues[c] += dot(own_low, g)
            own_dkeys[c] += dot(own_ds, q)
            first = self.first
            at = pl.multiple_of(c * tokens + first, SUB)
            row_live = lax.broadcasted_iota(jnp.int32, (SUB, HEAD), 0) + first < lengths[c]
            c_part = cosine[pl.ds(first, SUB), :]
            s_part = sine[pl.ds(first, SUB), :]
            for h in range(heads):
                cols = slice(h * HEAD, (h + 1) * HEAD)
                o = out[h * SUB : (h + 1) * SUB]
                out_ref[pl.ds(at, SUB), cols] = jnp.where(row_live, o, 0.0).astype(BF)
                d = dq[h * SUB : (h + 1) * SUB]
                turned = d * c_part - pltpu.roll(d, HEAD // 2, 1) * s_part
                ddelta[pl.ds(at, SUB), cols] = turned.astype(BF)
            span = pl.ds(at, SUB)
            pltpu.make_async_copy(out_ref.at[span], out_hbm.at[span], sems.at[0]).start()

    def group(used, i):
        chunks = [(at, min(CHUNK, used - at)) for at in range(0, used, CHUNK)] + [(n_prompt, tokens)]
        x, y = (Unit(i * PAIR + u, u, used) for u in range(PAIR))
        for at, size in chunks:
            x.score(at, size)
        x.scored()
        for at, size in chunks:
            x.weigh(at, size)
            y.score(at, size)
        x.weighed()
        y.scored()
        for at, size in chunks:
            x.differ(at, size)
            y.weigh(at, size)
        y.weighed()
        for at, size in chunks:
            y.differ(at, size)
        x.finish()
        y.finish()

    def alone(used, n):
        chunks = [(at, min(CHUNK, used - at)) for at in range(0, used, CHUNK)] + [(n_prompt, tokens)]
        x = Unit(n, 0, used)
        for at, size in chunks:
            x.score(at, size)
        x.scored()
        for at, size in chunks:
            x.weigh(at, size)
        x.weighed()
        for at, size in chunks:
            x.differ(at, size)
        x.finish()

    for used in range(SPAN, n_prompt + 1, SPAN):

        @pl.when(jnp.logical_and(count > used - SPAN, count <= used))
        def _(used=used):
            def step(i, carry):
                group(used, i)
                return carry

            lax.fori_loop(0, n_live // PAIR, step, 0)

            @pl.when(n_live % PAIR == 1)
            def _():
                alone(used, n_live - 1)

    copies = []
    for j in range(n_blocks):
        target = slots[prompt * n_blocks + j] // 2
        span = slice(j * tokens, (j + 1) * tokens)
        dprompt_ref[j, 0:tokens] = (dkeys[span] * inv_scale).astype(BF)
        dprompt_ref[j, tokens : 2 * tokens] = dvalues[span].astype(BF)
        block = dprompt_hbm.at[target, pl.ds(0, 2 * tokens)]
        copies.append(pltpu.make_async_copy(dprompt_ref.at[j], block, sems.at[3 + j]))
        copies[-1].start()
    for c in range(n_comp):
        down_ref[pl.ds(2 * c * tokens, tokens, 2), :] = own_dkeys[c] * inv_scale
        down_ref[pl.ds(2 * c * tokens + 1, tokens, 2), :] = own_dvalues[c]
    copies.append(pltpu.make_async_copy(down_ref, down_hbm, sems.at[2]))
    copies[-1].start()
    dd = ddelta[...]
    dup = dot(mid[...].T, dd)
    pack_rows(dup, dup.shape[0] // dup_ref.shape[0], dup_ref, 0)
    rest = dprompt_hbm.at[:, pl.ds(2 * tokens, dup_ref.shape[1])]
    copies.append(pltpu.make_async_copy(dup_ref, rest, sems.at[1]))
    copies[-1].start()
    split_halves(dot_nt(dd, up[...]), dmid_send, dmid_keep)
    for copy in copies:
        copy.wait()
    pltpu.make_async_copy(out_ref, out_hbm, sems.at[0]).wait()


def prepare_call(prompts, slots, hidden, down, stored, n_dp):
    rows = stored.shape[0] // 4
    return call(
        prepare,
        (
            *(pltpu.VMEM((hidden.shape[0] // 2, down.shape[0]), F32),) * 2,
            pltpu.HBM((n_dp, 2, rows, HEAD), BF),
        ),
        [SM] * 2 + [HBM] * 3,
        (VM, VM, HBM),
        12,
        [
            pltpu.VMEM(hidden.shape, BF),
            pltpu.VMEM(down.shape, BF),
            pltpu.VMEM(stored.shape, BF),
            pltpu.VMEM(stored.shape, F32),
            pltpu.VMEM((n_dp, 2, rows, HEAD), BF),
            pltpu.SemaphoreType.DMA((4,)),
        ],
    )(*in_hbm(prompts, slots, hidden, down, stored))


def attend(prompts, counts, lengths, slots, mid_kept, mid_other, base, up, gathered, g_rows, own, cosine, sine):
    n_tokens, width = base.shape
    n_comp = lengths.shape[0]
    tokens = n_tokens // n_comp
    rank = mid_kept.shape[1]
    n_dp = gathered.shape[0]
    grad_rows = rank // n_dp * width // HEAD
    n_prompt = slots.shape[0] // counts.shape[0] * tokens
    n_keys = n_prompt + tokens
    rows = width // HEAD * SUB
    prompts, counts, lengths, slots = in_hbm(prompts, counts, lengths, slots)
    g_rows, base = in_vmem(g_rows, base)
    up, *own, cosine, sine = in_hbm(up, *own, cosine, sine)
    return call(
        attention,
        (
            pltpu.HBM(base.shape, BF),
            *(pltpu.VMEM(mid_kept.shape, F32),) * 2,
            pltpu.HBM((n_dp, 2 * tokens + grad_rows, HEAD), BF),
            pltpu.HBM((2 * n_tokens, HEAD), F32),
        ),
        [SM] * 4 + [VM] * 3 + [HBM] + [VM] * 2 + [HBM] * 4,
        (HBM, VM, VM, HBM, HBM),
        44,
        [
            pltpu.SMEM((n_tokens // SUB,), jnp.int32),
            pltpu.VMEM(up.shape, BF),
            *(pltpu.VMEM(part.shape, BF) for part in own),
            pltpu.VMEM(cosine.shape, F32),
            pltpu.VMEM(sine.shape, F32),
            pltpu.VMEM((n_comp, HEAD, tokens), BF),
            pltpu.VMEM((n_comp, HEAD, tokens), BF),
            pltpu.VMEM((n_tokens, rank), BF),
            pltpu.VMEM((n_prompt, HEAD), BF),
            pltpu.VMEM((n_prompt, HEAD), BF),
            pltpu.VMEM((HEAD, n_prompt), BF),
            pltpu.VMEM((HEAD, n_prompt), BF),
            pltpu.VMEM((n_tokens // SUB, rows, HEAD), BF),
            pltpu.VMEM((PAIR, n_keys, rows), F32),
            pltpu.VMEM((PAIR, n_keys, rows), F32),
            pltpu.VMEM((PAIR, n_keys, rows), BF),
            pltpu.VMEM((PAIR, n_keys, rows), BF),
            pltpu.VMEM((n_prompt, HEAD), F32),
            pltpu.VMEM((n_prompt, HEAD), F32),
            pltpu.VMEM((n_comp, tokens, HEAD), F32),
            pltpu.VMEM((n_comp, tokens, HEAD), F32),
            pltpu.VMEM(base.shape, BF),
            pltpu.VMEM(base.shape, BF),
            pltpu.VMEM((n_prompt // tokens, 2 * tokens, HEAD), BF),
            pltpu.VMEM((2 * n_tokens, HEAD), F32),
            pltpu.VMEM((n_dp, grad_rows, HEAD), BF),
            pltpu.VMEM((SUB, width), BF),
            pltpu.SemaphoreType.DMA((3 + n_prompt // tokens,)),
            pltpu.SemaphoreType.DMA((5,)),
        ],
    )(prompts, counts, lengths, slots, mid_kept, mid_other, base, up, gathered, g_rows, *own, cosine, sine)


def down_gradient(dmid_kept, dmid_other, hidden, *refs):
    *out_refs, dmid, ddown = refs
    join_halves(dmid_kept, dmid_other, dmid)
    ddown[...] = dot(dmid[...].T, hidden[...])
    side = len(out_refs)
    part = ddown.shape[0] // side**2
    x = lax.rem(lax.axis_index("dp"), side)
    for k, out_ref in enumerate(out_refs):
        for y in range(side):
            owner = y * side + lax.rem(x + k, side)
            rows = ddown[pl.ds(pl.multiple_of(owner * part, part), part), :]
            pack_rows(rows, part, out_ref.at[pl.ds(y, 1)], 0)


def sum_along_x(*refs):
    side = len(refs) // 2
    got, out_refs = refs[:side], refs[side:]
    y = lax.div(lax.axis_index("dp"), side)
    for k, out_ref in enumerate(out_refs):
        row = lax.rem(y + k, side)
        total = got[0][row].astype(F32)
        for ref in got[1:]:
            total += ref[row].astype(F32)
        out_ref[...] = total.astype(BF)


def finish_down(*refs):
    *got, ddown_ref = refs
    part = ddown_ref.shape[0]
    total = got[0][...].astype(F32)
    for ref in got[1:]:
        total += ref[...].astype(F32)
    for k in range(ddown_ref.shape[1] // HEAD):
        ddown_ref[:, k * HEAD : (k + 1) * HEAD] = total[k * part : (k + 1) * part]


def finish_prompt(prompts, slots, got, dprompt_ref, dup_ref):
    n_dp = got.shape[0]
    rows = dprompt_ref.shape[0] // 4
    per_prompt = slots.shape[0] * 4 // prompts.shape[0]
    labels = stored_prompts(slots, lax.axis_index("dp"), per_prompt)
    for i in range(2):
        dk = jnp.zeros((rows, HEAD), F32)
        dv = jnp.zeros((rows, HEAD), F32)
        for e in range(n_dp):
            mine = prompts[e] == labels[i]
            dk += jnp.where(mine, got[e, 0:rows].astype(F32), 0.0)
            dv += jnp.where(mine, got[e, rows : 2 * rows].astype(F32), 0.0)
        dprompt_ref[pl.ds(2 * rows * i, rows, 2), :] = dk
        dprompt_ref[pl.ds(2 * rows * i + 1, rows, 2), :] = dv
    unpack_sum(got, dup_ref.shape[0], 2 * rows, dup_ref)


def along_x(side, k):
    return [(side * y + x, side * y + (x + k) % side) for y in range(side) for x in range(side)]


def along_y(side, k):
    return [(side * y + x, side * ((y + k) % side) + x) for y in range(side) for x in range(side)]


def sum_over_tensor(send, keep, sent, beside=None):
    n = lax.axis_size("tensor")
    swap = [(i, i ^ 1) for i in range(n)]
    pair = (keep + lax.ppermute(send, "tensor", swap)).astype(sent)
    got = [lax.ppermute(pair, "tensor", [(i, (i + k) % n) for i in range(n)]) for k in range(2, n, 2)]
    done = None
    if beside is not None:
        got, done = lax.optimization_barrier((got, beside(pair)))
    total = pair.astype(F32)
    for part in got:
        total += part.astype(F32)
    kept = total.astype(BF)
    return kept, lax.ppermute(kept, "tensor", swap), done


def local(
    hidden,
    base,
    own_kv,
    prompt_kv,
    down,
    up,
    grad,
    prompts,
    counts,
    lengths,
    slots,
):
    n_tokens, width = hidden.shape
    n_comp = lengths.shape[0]
    tokens = n_tokens // n_comp
    rank = down.shape[0]
    n_dp = lax.axis_size("dp")
    stored = prompt_kv.reshape(-1, HEAD)
    own = own_kv.reshape(-1, HEAD)

    mid_send, mid_keep, send = prepare_call(prompts, slots, hidden, down, stored, n_dp)
    gathered = lax.all_to_all(send, "dp", 0, 0)

    rows = width // HEAD * SUB

    def beside(pair):
        after, _ = lax.optimization_barrier(((grad, own), pair))
        return call(
            prepare_own,
            (
                pltpu.VMEM((n_tokens // SUB, rows, HEAD), BF),
                *(pltpu.HBM((n_comp, tokens, HEAD), BF),) * 2,
                pltpu.VMEM(base.shape, BF),
                *(pltpu.HBM((tokens, HEAD), F32),) * 2,
            ),
            [SM] * 3 + [VM] * 2 + [HBM],
            (VM,) * 6,
            12,
            [pltpu.VMEM(own.shape, F32), pltpu.SemaphoreType.DMA],
        )(*in_hbm(prompts, counts, lengths, *after, base))

    mid_kept, mid_other, (g_rows, *own_parts, base, cosine, sine) = sum_over_tensor(mid_send, mid_keep, F32, beside)
    out, dmid_send, dmid_keep, dprompt, down_own = attend(
        prompts, counts, lengths, slots, mid_kept, mid_other, base, up, gathered, g_rows, own_parts, cosine, sine
    )
    grad_rows = rank // n_dp * width // HEAD
    got = lax.all_to_all(dprompt, "dp", 0, 0)
    dmid_kept, dmid_other, _ = sum_over_tensor(dmid_send, dmid_keep, BF)
    grad_shape = shape((rank // n_dp, width), F32)
    side = math.isqrt(n_dp)
    pieces = call(
        down_gradient,
        (shape((side, grad_rows, HEAD), BF),) * side,
        [VM] * 3,
        (VM,) * side,
        8,
        [pltpu.VMEM((n_tokens, rank), BF), pltpu.VMEM((rank, width), F32)],
    )(dmid_kept, dmid_other, hidden)
    pieces = [pieces[0], *(lax.ppermute(pieces[k], "dp", along_x(side, k)) for k in range(1, side))]
    pieces = call(sum_along_x, (shape((grad_rows, HEAD), BF),) * side, [VM] * side, (VM,) * side, 4)(*pieces)
    pieces = [pieces[0], *(lax.ppermute(pieces[k], "dp", along_y(side, k)) for k in range(1, side))]
    dprompt, dup = call(
        finish_prompt,
        (shape(stored.shape, F32), grad_shape),
        [SM] * 2 + [VM],
        (VM,) * 2,
        6,
    )(prompts, slots, got)
    pieces, dprompt, dup = lax.optimization_barrier((pieces, dprompt, dup))
    ddown = call(finish_down, grad_shape, [VM] * side, VM, 4)(*pieces)
    return (
        out,
        ddown,
        dup,
        dprompt.reshape(prompt_kv.shape),
        down_own.reshape(own_kv.shape),
    )


def solution(mesh):
    placed = (
        P("dp", "tensor"),
        P("dp", "tensor"),
        P("dp", None, "tensor", None),
        P("dp", None, "tensor", None),
        P(None, "tensor"),
        P(None, "tensor"),
        P("dp", "tensor"),
        P(),
        P(),
        P("dp"),
        P(),
    )
    return jax.shard_map(
        local,
        mesh=mesh,
        in_specs=placed,
        out_specs=(
            P("dp", "tensor"),
            P("dp", "tensor"),
            P("dp", "tensor"),
            P("dp", None, "tensor", None),
            P("dp", None, "tensor", None),
        ),
        check_vma=False,
    )
```
